512 devices in a mesh: tm: 32 (over z, y_lo), series: 16 (over x, y_hi, core).
Axes of the slice: x: 4, y: 8 (y_hi: 2, y_lo: 4; y = y_hi * 4 + y_lo), z: 8, core: 2. Of those that a mesh axis runs over, the one named last changes fastest.
Arguments:
- series_factors: bfloat16 [16384, 256], P(('series', 'tm')), may hold values from -1.5 to 1.5
- time_factors: bfloat16 [16384, 256], P(('tm', 'series')), may hold values from -1.5 to 1.5
- tile_values: bfloat16 [4096, 256, 256], P(('tm', 'series')), may hold values from -6 to 6
- tile_blocks: int32 [4096, 2], P(('tm', 'series')), may hold values from 0 to 63, as said below
- tile_counts: int32 [512], P(('tm', 'series')), may hold values from 1 to 8, as said below
- lags: int32 [96], replicated, may hold values from 1 to 168, as said below
- lag_weights: float32 [96, 256], replicated, may hold values from -0.4 to 0.4
Outputs:
- grad_series: float32 [16384, 256], P(('series', 'tm'))
- grad_time: float32 [16384, 256], P(('tm', 'series'))
The draws below stay inside these ranges and needn't reach their ends.
Inputs may be any that keep to these rules, and one draw needn't show every extreme that they name: `tile_blocks`: row r names a series block in [4 s, 4 (s + 1)) and a time block in [2 t, 2 (t + 1)), where r // 8 = 16 t + s. `tile_counts`: at least one group lists 8 blocks. `lags`: Distinct, rising, and include 1 and 168.
All inputs are finite; a program needn't handle non-finite values.
Results may differ from the reference program's by a relative error of at most 0.0025.
Values may be sent and summed in bfloat16 or wider, within the bound.
A program may use at most 64 MiB of HBM per device.

```python
import jax
import jax.numpy as jnp
from jax import lax

K = 256
TILE = 256
LMAX = 168
LAGS = 96
SBLOCKS = 4
TBLOCKS = 2
CAP = 8
SERIES_ALL = 16384
STEPS_ALL = 16384
N_SERIES = 16
DEVICES = 512


def draw_tile_counts(key, part):
    key = jax.random.fold_in(key, 11)
    first, second, third = jax.random.split(key, 3)
    left = jax.random.randint(first, (DEVICES,), 1, CAP + 1)
    right = jax.random.randint(second, (DEVICES,), 1, CAP + 1)
    busiest = jax.random.randint(third, (), 0, DEVICES)
    lower = jnp.minimum(left, right)
    return jnp.where(jnp.arange(DEVICES) == busiest, CAP, lower).astype(jnp.int32)


def draw_tile_blocks(key, part):
    key = jax.random.fold_in(key, 23)
    first, second = jax.random.split(key, 2)
    groups = jnp.arange(DEVICES * CAP) // CAP
    slab = groups // N_SERIES
    block = groups % N_SERIES
    series_block = block * SBLOCKS + jax.random.randint(first, (DEVICES * CAP,), 0, SBLOCKS)
    time_block = slab * TBLOCKS + jax.random.randint(second, (DEVICES * CAP,), 0, TBLOCKS)
    return jnp.stack([series_block, time_block], axis=1).astype(jnp.int32)


def draw_lags(key, part):
    key = jax.random.fold_in(key, 37)
    inner = jax.random.permutation(key, LMAX - 2) + 2
    chosen = jnp.concatenate([jnp.array([1, LMAX]), inner[:LAGS - 2]])
    return jnp.sort(chosen).astype(jnp.int32)


def shard_levels(key, extent, cuts, low, top_value):
    def one(axis_at, parts):
        steps = jax.random.uniform(jax.random.fold_in(jax.random.fold_in(key, 6), axis_at), (parts,), jnp.float32, low / len(cuts), top_value / len(cuts))
        return jnp.repeat(jnp.exp(steps), extent[axis_at] // parts).reshape((-1,) + (1,) * (len(extent) - axis_at - 1))

    factor_of = one(*cuts[0])
    for cut in cuts[1:]:
        factor_of = factor_of * one(*cut)
    return factor_of


def noise(own_key, shape, spread, reach, cuts=(), kind=jnp.bfloat16):
    entries = spread * jax.random.normal(own_key, shape, jnp.float32)
    if cuts:
        entries = entries * shard_levels(own_key, shape, cuts, -0.22, 0.18)
    return jnp.clip(entries, -reach, reach).astype(kind)


def setup_inputs(seed: int = 0) -> dict:
    seeds = jax.random.split(jax.random.key(seed), 8)
    series_factors = noise(seeds[0], (SERIES_ALL, K), 0.25, 1.5, ((0, 512),))
    time_factors = noise(seeds[1], (STEPS_ALL, K), 0.25, 1.5, ((0, 512),))
    tile_values = noise(seeds[2], (DEVICES * CAP, TILE, TILE), 1.0, 6.0, ((0, 512),))
    tile_blocks = draw_tile_blocks(jax.random.fold_in(seeds[7], 71), 0)
    tile_counts = draw_tile_counts(jax.random.fold_in(seeds[7], 71), 0)
    lags = draw_lags(jax.random.fold_in(seeds[7], 71), 0)
    lag_weights = noise(seeds[6], (LAGS, K), 0.1, 0.4, (), jnp.float32)
    return {"series_factors": series_factors, "time_factors": time_factors, "tile_values": tile_values, "tile_blocks": tile_blocks, "tile_counts": tile_counts, "lags": lags, "lag_weights": lag_weights}


def reference(series_factors, time_factors, tile_values, tile_blocks, tile_counts, lags, lag_weights):
    tile = tile_values.shape[1]
    zero_index = jnp.zeros((), jnp.int32)

    def one_slot(slot, carry):
        grad_rows, grad_steps = carry
        first = (tile_blocks[slot, 0] * tile).astype(jnp.int32)
        second = (tile_blocks[slot, 1] * tile).astype(jnp.int32)
        f_rows = lax.dynamic_slice_in_dim(series_factors, first, tile, 0)
        x_rows = lax.dynamic_slice_in_dim(time_factors, second, tile, 0)
        pred = jnp.dot(f_rows, x_rows.T, preferred_element_type=jnp.float32)
        resid = (tile_values[slot].astype(jnp.float32) - pred).astype(jnp.bfloat16)
        part_f = -jnp.dot(resid, x_rows, preferred_element_type=jnp.float32) * (1.0 / tile)
        part_x = -jnp.dot(resid.T, f_rows, preferred_element_type=jnp.float32) * (1.0 / tile)
        old_f = lax.dynamic_slice_in_dim(grad_rows, first, tile, 0)
        old_x = lax.dynamic_slice_in_dim(grad_steps, second, tile, 0)
        grad_rows = lax.dynamic_update_slice(grad_rows, old_f + part_f, (first, zero_index))
        grad_steps = lax.dynamic_update_slice(grad_steps, old_x + part_x, (second, zero_index))
        return grad_rows, grad_steps

    def one_group(group, carry):
        begin = group * CAP
        return lax.fori_loop(begin, begin + tile_counts[group], one_slot, carry)

    start = (jnp.zeros(series_factors.shape, jnp.float32), jnp.zeros(time_factors.shape, jnp.float32))
    data_series, data_time = lax.fori_loop(0, DEVICES, one_group, start)

    steps_all = time_factors.shape[0]
    factors = time_factors.astype(jnp.float32)
    padded = jnp.concatenate([jnp.zeros((LMAX, K), jnp.float32), factors], axis=0)

    def add_past(m, acc):
        begin = (LMAX - lags[m]).astype(jnp.int32)
        return acc + lag_weights[m] * lax.dynamic_slice_in_dim(padded, begin, steps_all, 0)

    pred_ar = lax.fori_loop(0, LAGS, add_past, jnp.zeros((steps_all, K), jnp.float32))
    position = jnp.arange(steps_all)[:, None]
    err = jnp.where(position >= LMAX, factors - pred_ar, 0.0)
    padded_err = jnp.concatenate([err, jnp.zeros((LMAX, K), jnp.float32)], axis=0)

    def add_future(m, acc):
        begin = lags[m].astype(jnp.int32)
        return acc + lag_weights[m] * lax.dynamic_slice_in_dim(padded_err, begin, steps_all, 0)

    ahead = lax.fori_loop(0, LAGS, add_future, jnp.zeros((steps_all, K), jnp.float32))
    ar_grad = err - ahead
    grad_series = data_series + 0.5 * series_factors.astype(jnp.float32)
    grad_time = data_time + 0.5 * factors + 2.0 * ar_grad
    return grad_series, grad_time
```

```python
import jax
import jax.numpy as jnp
from jax import lax
from jax.experimental import pallas as pl
from jax.experimental.pallas import tpu as pltpu
from jax.sharding import PartitionSpec as P

LMAX = 168
NZ, NY, NX, NH, NC = 8, 4, 4, 2, 2
ROWS = 32
TILE = 256
HALF = 128
SB = NZ * NY * ROWS // TILE
TB = NX * NH * NC * ROWS // TILE
SLAB = NX * NH * NC
HALO = 6
ERR = ROWS + LMAX
MESH = pl.DeviceIdType.MESH
F32 = jnp.float32
BF16 = jnp.bfloat16


def contract(a, b, da, db):
    return lax.dot_general(a, b, (((da,), (db,)), ((), ())), preferred_element_type=F32)


def kernel(
    sf, tf, values, blocks, counts, lags, weights, out_s, out_t,
    tv, fa, fb, xw, before, after, acc_s, acc_t, pa, pb, pt, za, yb, qa, qb, ya, zb,
    rc, qc, rx, qx, rh, wf, eb, ww, local_sem,
    fa_y, fa_z, fb_z, fb_y, x_h, x_x, x_c, halo, sa_z, sa_y, sb_y, sb_z, t_c, t_x, t_h,
):
    tm, s = lax.axis_index("tm"), lax.axis_index("series")
    z, y = tm // NY, tm % NY
    x, h, c = s // (NH * NC), (s // NC) % NH, s % NC

    def at_z(i):
        return (i * NY + y, s)

    def at_y(i):
        return (z * NY + i, s)

    def at_x(i):
        return (tm, i * (NH * NC) + h * NC + c)

    other_h = (tm, x * (NH * NC) + (1 - h) * NC + c)
    other_c = (tm, x * (NH * NC) + h * NC + (1 - c))

    load_values = pltpu.make_async_copy(values, tv, local_sem)
    load_values.start()

    takes_past = (s < HALO) & (tm > 0)
    gives_past = (s < HALO) & (tm < NZ * NY - 1)
    takes_next = (s >= SLAB - HALO) & (tm < NZ * NY - 1)
    gives_next = (s >= SLAB - HALO) & (tm > 0)

    barrier = pltpu.get_barrier_semaphore()

    def greet(device):
        pl.semaphore_signal(barrier, inc=1, device_id=device, device_id_type=MESH)

    for d in range(1, NY):
        greet(at_y((y + d) % NY))
    for d in range(1, NZ):
        greet(at_z((z + d) % NZ))
    for d in range(1, NX):
        greet(at_x((x + d) % NX))
    greet(other_h)
    greet(other_c)

    @pl.when(takes_past)
    def _():
        greet((tm - 1, s))

    @pl.when(takes_next)
    def _():
        greet((tm + 1, s))

    fa[z, y] = sf[:, :HALF]
    fb[z, y] = sf[:, HALF:]
    xw[s] = tf[...]
    more = jnp.where(gives_past | gives_next, 1, 0)
    pl.semaphore_wait(barrier, NY - 1 + NZ - 1 + NX - 1 + 2 + more)

    sent = []

    def copy(src, dst, sems, i, device):
        return pltpu.make_async_remote_copy(
            src_ref=src, dst_ref=dst, send_sem=sems.at[0, i], recv_sem=sems.at[1, i],
            device_id=device, device_id_type=MESH,
        )

    def send(src, dst, sems, i, device):
        one = copy(src, dst, sems, i, device)
        one.start()
        sent.append(one)

    def arrive(dst, sems, i, device):
        copy(dst, dst, sems, i, device).wait_recv()

    send(xw.at[s], xw.at[s], x_h, 0, other_h)
    for d in range(1, NY):
        send(fa.at[z, y], fa.at[z, y], fa_y, d - 1, at_y((y + d) % NY))
    for d in range(1, NZ):
        send(fb.at[z, y], fb.at[z, y], fb_z, d - 1, at_z((z + d) % NZ))

    def slab_block(i, j, k):
        return i * (NH * NC) + j * NC + k

    arrive(xw.at[slab_block(x, 1 - h, c)], x_h, 0, other_h)
    for d in range(1, NX):
        for j in range(NH):
            part = xw.at[slab_block(x, j, c)]
            send(part, part, x_x, (d - 1) * NH + j, at_x((x + d) % NX))

    for d in range(1, NY):
        arrive(fa.at[z, (y + NY - d) % NY], fa_y, d - 1, at_y((y + d) % NY))
    for d in range(1, NZ):
        send(fa.at[z], fa.at[z], fa_z, d - 1, at_z((z + d) % NZ))
    for d in range(1, NZ):
        arrive(fb.at[(z + NZ - d) % NZ, y], fb_z, d - 1, at_z((z + d) % NZ))
    for d in range(1, NY):
        send(fb.at[:, y], fb.at[:, y], fb_y, d - 1, at_y((y + d) % NY))

    for d in range(1, NX):
        for j in range(NH):
            got = xw.at[slab_block((x + NX - d) % NX, j, c)]
            arrive(got, x_x, (d - 1) * NH + j, at_x((x + d) % NX))
    for i in range(NX):
        for j in range(NH):
            part = xw.at[slab_block(i, j, c)]
            send(part, part, x_c, i * NH + j, other_c)
    for i in range(NX):
        for j in range(NH):
            arrive(xw.at[slab_block(i, j, 1 - c)], x_c, i * NH + j, other_c)

    give_past = copy(xw.at[pl.ds(SLAB - HALO, HALO)], before, halo, 0, (tm + 1, s))
    give_next = copy(xw.at[pl.ds(0, HALO)], after, halo, 1, (tm - 1, s))
    take_past = copy(before, before, halo, 0, (tm - 1, s))
    take_next = copy(after, after, halo, 1, (tm + 1, s))

    @pl.when(gives_past)
    def _():
        give_past.start()

    @pl.when(gives_next)
    def _():
        give_next.start()

    acc_s[...] = jnp.zeros_like(acc_s)
    acc_t[...] = jnp.zeros_like(acc_t)
    ww[0] = weights[:, :HALF]
    ww[1] = weights[:, HALF:]

    load_values.wait()
    for d in range(1, NZ):
        arrive(fa.at[(z + NZ - d) % NZ], fa_z, d - 1, at_z((z + d) % NZ))
    for d in range(1, NY):
        arrive(fb.at[:, (y + NY - d) % NY], fb_y, d - 1, at_y((y + d) % NY))

    used = counts[0]
    per_z = TILE // (NY * ROWS)
    per_x = TILE // ROWS

    def slot(m, carry):
        at_series = lax.rem(blocks[m, 0], SB)
        at_time = lax.rem(blocks[m, 1], TB)
        f_left = fa[pl.ds(at_series * per_z, per_z)].reshape(TILE, HALF)
        f_right = fb[pl.ds(at_series * per_z, per_z)].reshape(TILE, HALF)
        f = jnp.concatenate([f_left, f_right], axis=1)
        t = xw[pl.ds(at_time * per_x, per_x)].reshape(TILE, TILE)
        pred = contract(f, t, 1, 1)
        resid = jnp.where(m < used, tv[m].astype(F32) - pred, 0.0).astype(BF16)
        part_s = contract(resid, t, 1, 0)
        part_t = contract(resid, f, 0, 0)
        for k in range(SB):
            acc_s[k] += jnp.where(at_series == k, part_s, 0.0)
        for k in range(TB):
            acc_t[k] += jnp.where(at_time == k, part_t, 0.0)
        return carry

    lax.fori_loop(0, values.shape[0], slot, 0)

    scale = -1.0 / TILE
    for k in range(TB):
        part = (acc_t[k] * scale).astype(BF16).reshape(per_x, ROWS, TILE)
        pt[pl.ds(k * per_x, per_x)] = part
    for i in range(NX):
        for j in range(NH):
            n = i * NH + j
            send(pt.at[n * NC + (1 - c)], rc.at[n], t_c, n, other_c)
    for k in range(SB):
        part = (acc_s[k] * scale).astype(BF16).reshape(per_z, NY, ROWS, TILE)
        pa[pl.ds(k * per_z, per_z)] = part[..., :HALF]
        pb[pl.ds(k * per_z, per_z)] = part[..., HALF:]
    for d in range(1, NZ):
        there = (z + d) % NZ
        send(pa.at[there], za.at[d - 1], sa_z, d - 1, at_z(there))
    for d in range(1, NY):
        there = (y + d) % NY
        send(pb.at[:, there], yb.at[d - 1], sb_y, d - 1, at_y(there))

    def widen(rows, first):
        rows = rows.astype(F32).reshape(-1, TILE)
        wf[0, pl.ds(first * ROWS, rows.shape[0])] = rows[:, :HALF]
        wf[1, pl.ds(first * ROWS, rows.shape[0])] = rows[:, HALF:]

    nothing = jnp.zeros((HALO, ROWS, TILE), BF16)
    widen(xw[...], HALO)

    @pl.when(takes_past)
    def _():
        take_past.wait_recv()
        widen(before[...], 0)

    @pl.when(jnp.logical_not(takes_past))
    def _():
        widen(nothing, 0)

    @pl.when(takes_next)
    def _():
        take_next.wait_recv()
        widen(after[...], HALO + SLAB)

    @pl.when(jnp.logical_not(takes_next))
    def _():
        widen(nothing, HALO + SLAB)

    steps = tm * (SLAB * ROWS) + s * ROWS + lax.broadcasted_iota(jnp.int32, (ERR, HALF), 0)
    inside = (steps >= LMAX) & (steps < NZ * NY * SLAB * ROWS)

    base = (HALO + s) * ROWS

    def errors(side):
        def add(m, total):
            w = ww[side, pl.ds(m, 1), :]
            return total + w * wf[side, pl.ds(base - lags[m], ERR), :]

        pred = lax.fori_loop(0, lags.shape[0], add, jnp.zeros((ERR, HALF), F32))
        eb[side] = jnp.where(inside, wf[side, pl.ds(pl.multiple_of(base, ROWS), ERR), :] - pred, 0.0)

    def ahead(side):
        def add(m, total):
            w = ww[side, pl.ds(m, 1), :]
            return total + w * eb[side, pl.ds(lags[m], ROWS), :]

        return lax.fori_loop(0, lags.shape[0], add, jnp.zeros((ROWS, HALF), F32))

    errors(0)

    for n in range(NX * NH):
        arrive(rc.at[n], t_c, n, other_c)
    for n in range(NX * NH):
        qc[n] = pt[n * NC + c].astype(F32) + rc[n].astype(F32)
    for d in range(1, NX):
        there = (x + d) % NX
        send(qc.at[pl.ds(there * NH, NH)], rx.at[d - 1], t_x, d - 1, at_x(there))

    errors(1)

    for d in range(1, NX):
        arrive(rx.at[d - 1], t_x, d - 1, at_x((x + d) % NX))
    qx[...] = qc[pl.ds(x * NH, NH)] + rx[0] + rx[1] + rx[2]
    send(qx.at[1 - h], rh, t_h, 0, other_h)

    for d in range(1, NY):
        arrive(yb.at[d - 1], sb_y, d - 1, at_y((y + d) % NY))
    total = pb[:, y].astype(F32)
    for d in range(1, NY):
        total = total + yb[d - 1].astype(F32)
    qb[...] = total
    for d in range(1, NZ):
        there = (z + d) % NZ
        send(qb.at[there], zb.at[d - 1], sb_z, d - 1, at_z(there))
    for d in range(1, NZ):
        arrive(za.at[d - 1], sa_z, d - 1, at_z((z + d) % NZ))
    total = pa[z].astype(F32)
    for d in range(1, NZ):
        total = total + za[d - 1].astype(F32)
    qa[...] = total
    for d in range(1, NY):
        there = (y + d) % NY
        send(qa.at[there], ya.at[d - 1], sa_y, d - 1, at_y(there))

    grads = [2.0 * (eb[side, pl.ds(0, ROWS), :] - ahead(side)) for side in range(2)]
    arrive(rh, t_h, 0, other_h)
    own = qx[h] + rh[...] + 0.5 * tf[...].astype(F32)
    out_t[...] = own + jnp.concatenate(grads, axis=1)

    for d in range(1, NZ):
        arrive(zb.at[d - 1], sb_z, d - 1, at_z((z + d) % NZ))
    right = qb[z]
    for d in range(1, NZ):
        right = right + zb[d - 1]
    for d in range(1, NY):
        arrive(ya.at[d - 1], sa_y, d - 1, at_y((y + d) % NY))
    left = qa[y]
    for d in range(1, NY):
        left = left + ya[d - 1]
    out_s[...] = jnp.concatenate([left, right], axis=1) + 0.5 * sf[...].astype(F32)

    for one in sent:
        one.wait_send()

    @pl.when(gives_past)
    def _():
        give_past.wait_send()

    @pl.when(gives_next)
    def _():
        give_next.wait_send()


def shards(series_factors, time_factors, tile_values, tile_blocks, tile_counts, lags, lag_weights):
    vmem = pl.BlockSpec(memory_space=pltpu.VMEM)
    smem = pl.BlockSpec(memory_space=pltpu.SMEM)
    slots = tile_values.shape[0]
    own = jax.ShapeDtypeStruct((ROWS, TILE), F32)

    def pair(n):
        return pltpu.SemaphoreType.DMA((2, n))

    return tuple(
        pl.pallas_call(
            kernel,
            out_shape=(own, own),
            in_specs=[vmem, vmem, pl.BlockSpec(memory_space=pl.ANY), smem, smem, smem, vmem],
            out_specs=(vmem, vmem),
            scratch_shapes=[
                pltpu.VMEM((slots, TILE, TILE), BF16),
                pltpu.VMEM((NZ, NY, ROWS, HALF), BF16),
                pltpu.VMEM((NZ, NY, ROWS, HALF), BF16),
                pltpu.VMEM((SLAB, ROWS, TILE), BF16),
                pltpu.VMEM((HALO, ROWS, TILE), BF16),
                pltpu.VMEM((HALO, ROWS, TILE), BF16),
                pltpu.VMEM((SB, TILE, TILE), F32),
                pltpu.VMEM((TB, TILE, TILE), F32),
                pltpu.VMEM((NZ, NY, ROWS, HALF), BF16),
                pltpu.VMEM((NZ, NY, ROWS, HALF), BF16),
                pltpu.VMEM((SLAB, ROWS, TILE), BF16),
                pltpu.VMEM((NZ - 1, NY, ROWS, HALF), BF16),
                pltpu.VMEM((NY - 1, NZ, ROWS, HALF), BF16),
                pltpu.VMEM((NY, ROWS, HALF), F32),
                pltpu.VMEM((NZ, ROWS, HALF), F32),
                pltpu.VMEM((NY - 1, ROWS, HALF), F32),
                pltpu.VMEM((NZ - 1, ROWS, HALF), F32),
                pltpu.VMEM((NX * NH, ROWS, TILE), BF16),
                pltpu.VMEM((NX * NH, ROWS, TILE), F32),
                pltpu.VMEM((NX - 1, NH, ROWS, TILE), F32),
                pltpu.VMEM((NH, ROWS, TILE), F32),
                pltpu.VMEM((ROWS, TILE), F32),
                pltpu.VMEM((2, (SLAB + 2 * HALO) * ROWS, HALF), F32),
                pltpu.VMEM((2, ERR, HALF), F32),
                pltpu.VMEM((2, *lags.shape, HALF), F32),
                pltpu.SemaphoreType.DMA,
                pair(NY - 1), pair(NZ - 1), pair(NZ - 1), pair(NY - 1),
                pair(1), pair((NX - 1) * NH), pair(NX * NH), pair(2),
                pair(NZ - 1), pair(NY - 1), pair(NY - 1), pair(NZ - 1),
                pair(NX * NH), pair(NX - 1), pair(1),
            ],
            compiler_params=pltpu.CompilerParams(
                collective_id=0, has_side_effects=True, vmem_limit_bytes=40 * 2**20
            ),
            cost_estimate=pl.CostEstimate(
                flops=slots * 6 * TILE**3, bytes_accessed=slots * 2 * TILE**2, transcendentals=0
            ),
        )(series_factors, time_factors, tile_values, tile_blocks, tile_counts, lags, lag_weights)
    )


def solution(mesh):
    placed = (
        P(("series", "tm"), None),
        P(("tm", "series"), None),
        P(("tm", "series"), None, None),
        P(("tm", "series"), None),
        P(("tm", "series")),
        P(),
        P(),
    )
    return jax.shard_map(
        shards,
        mesh=mesh,
        in_specs=placed,
        out_specs=(P(("series", "tm"), None), P(("tm", "series"), None)),
        check_vma=False,
    )
```

```python
import jax
import jax.numpy as jnp
from jax import lax
from jax.experimental import pallas as pl
from jax.experimental.pallas import tpu as pltpu
from jax.sharding import PartitionSpec as P

LMAX = 168
NZ, NY, NX, NH, NC = 8, 4, 4, 2, 2
ROWS = 32
TILE = 256
HALF = 128
SB = NZ * NY * ROWS // TILE
TB = NX * NH * NC * ROWS // TILE
SLAB = NX * NH * NC
NEAR = [(i, j) for i in range(NX) for j in range(NC) if i + j]
HALO = 6
ERR = ROWS + LMAX
MESH = pl.DeviceIdType.MESH
F32 = jnp.float32
BF16 = jnp.bfloat16


def contract(a, b, da, db):
    return lax.dot_general(a, b, (((da,), (db,)), ((), ())), preferred_element_type=F32)


def kernel(
    sf_in, tf_in, values, blocks_in, counts_in, lags_in, weights_in, out,
    sf, tf, blocks, counts, lags, weights, tv, fa, fb, xw, before, after, acc_s, acc_t, pa, pb, pt, za, yb, qa, qb, ya, zb,
    rx, qx, rh, wf, eb, ww, local_sem,
    fa_y, fa_z, fb_z, fb_y, x_h, x_x, halo, sa_z, sa_y, sb_y, sb_z, t_x, t_h,
):
    tm, s = lax.axis_index("tm"), lax.axis_index("series")
    z, y = tm // NY, tm % NY
    x, h, c = s // (NH * NC), s // NC % NH, s % NC
    s_far = s + NC * (1 - 2 * h)

    def at_z(i):
        return (i * NY + y, s)

    def at_y(i):
        return (z * NY + i, s)

    def near(i, j):
        return (x + i) % NX * NH, (c + j) % NC

    def at_near(i, j):
        row, core = near(i, j)
        return (tm, (row + h) * NC + core)

    def from_near(i, j):
        return near(NX - i, NC - j)

    takes_past = (s < HALO) & (tm > 0)
    gives_past = (s < HALO) & (tm < NZ * NY - 1)
    takes_next = (s >= SLAB - HALO) & (tm < NZ * NY - 1)
    gives_next = (s >= SLAB - HALO) & (tm > 0)

    barrier = pltpu.get_barrier_semaphore()

    def greet(device):
        pl.semaphore_signal(barrier, inc=1, device_id=device, device_id_type=MESH)

    for d in range(1, NY):
        greet(at_y((y + d) % NY))
    for d in range(1, NZ):
        greet(at_z((z + d) % NZ))
    for i, j in NEAR:
        greet(at_near(i, j))
    greet((tm, s_far))

    @pl.when(takes_past)
    def _():
        greet((tm - 1, s))

    @pl.when(takes_next)
    def _():
        greet((tm + 1, s))

    loads = [
        pltpu.make_async_copy(src, dst, local_sem.at[i])
        for i, (src, dst) in enumerate(
            [(tf_in, tf), (sf_in, sf), (values, tv), (weights_in, weights), (lags_in, lags), (blocks_in, blocks), (counts_in, counts)]
        )
    ]
    for one in loads:
        one.start()

    loads[0].wait()
    loads[1].wait()
    fa[z, y] = sf[:, :HALF]
    fb[z, y] = sf[:, HALF:]
    xw[x * NH + h, c] = tf[...]
    more = jnp.where(gives_past | gives_next, 1, 0)
    pl.semaphore_wait(barrier, NY - 1 + NZ - 1 + len(NEAR) + 1 + more)

    sent = []

    def copy(src, dst, sems, i, device):
        return pltpu.make_async_remote_copy(
            src_ref=src, dst_ref=dst, send_sem=sems.at[0, i], recv_sem=sems.at[1, i],
            device_id=device, device_id_type=MESH,
        )

    def send(src, dst, sems, i, device):
        one = copy(src, dst, sems, i, device)
        one.start()
        sent.append(one)

    def arrive(dst, sems, i, device):
        copy(dst, dst, sems, i, device).wait_recv()

    send(xw.at[x * NH + h, c], xw.at[x * NH + h, c], x_h, 0, (tm, s_far))
    for d in range(1, NY):
        send(fa.at[z, y], fa.at[z, y], fa_y, d - 1, at_y((y + d) % NY))
    for d in range(1, NZ):
        send(fb.at[z, y], fb.at[z, y], fb_z, d - 1, at_z((z + d) % NZ))

    for d in range(1, NY):
        arrive(fa.at[z, (y + NY - d) % NY], fa_y, d - 1, at_y((y + d) % NY))
    for d in range(1, NZ):
        send(fa.at[z], fa.at[z], fa_z, d - 1, at_z((z + d) % NZ))
    for d in range(1, NZ):
        arrive(fb.at[(z + NZ - d) % NZ, y], fb_z, d - 1, at_z((z + d) % NZ))
    for d in range(1, NY):
        send(fb.at[:, y], fb.at[:, y], fb_y, d - 1, at_y((y + d) % NY))

    arrive(xw.at[x * NH + 1 - h, c], x_h, 0, (tm, s_far))
    part = xw.at[pl.ds(x * NH, NH), c]
    for n, (i, j) in enumerate(NEAR):
        send(part, part, x_x, n, at_near(i, j))
    for one in loads[2:]:
        one.wait()
    ww[0] = weights[:, :HALF]
    ww[1] = weights[:, HALF:]
    for n, (i, j) in enumerate(NEAR):
        row, core = from_near(i, j)
        arrive(xw.at[pl.ds(row, NH), core], x_x, n, at_near(i, j))
    give_past = copy(xw.at[pl.ds(SLAB // NC - HALO // NC, HALO // NC)], before, halo, 0, (tm + 1, s))
    give_next = copy(xw.at[pl.ds(0, HALO // NC)], after, halo, 1, (tm - 1, s))
    take_past = copy(before, before, halo, 0, (tm - 1, s))
    take_next = copy(after, after, halo, 1, (tm + 1, s))

    @pl.when(gives_past)
    def _():
        give_past.start()

    @pl.when(gives_next)
    def _():
        give_next.start()

    for d in range(1, NZ):
        arrive(fa.at[(z + NZ - d) % NZ], fa_z, d - 1, at_z((z + d) % NZ))
    for d in range(1, NY):
        arrive(fb.at[:, (y + NY - d) % NY], fb_y, d - 1, at_y((y + d) % NY))

    used = counts[0]
    per_z = TILE // (NY * ROWS)
    per_x = TILE // ROWS

    series_of, time_of = [], []
    for m in range(values.shape[0]):
        at_series = lax.rem(blocks[0, m], SB)
        at_time = lax.rem(blocks[1, m], TB)
        series_of.append(at_series)
        time_of.append(at_time)
        f_left = fa[pl.ds(at_series * per_z, per_z)].reshape(TILE, HALF)
        f_right = fb[pl.ds(at_series * per_z, per_z)].reshape(TILE, HALF)
        f = jnp.concatenate([f_left, f_right], axis=1)
        t = xw[pl.ds(at_time * (per_x // NC), per_x // NC)].reshape(TILE, TILE)
        pred = contract(f, t, 1, 1)
        resid = jnp.where(m < used, tv[m].astype(F32) - pred, 0.0).astype(BF16)
        acc_s[m] = contract(resid, t, 1, 0)
        acc_t[m] = contract(resid, f, 0, 0)

    scale = -1.0 / TILE
    rows_at_once = 64

    def gathered(acc, places, k, piece):
        total = jnp.zeros((rows_at_once, TILE), F32)
        for m, place in enumerate(places):
            total = total + jnp.where(place == k, acc[m, pl.ds(pl.multiple_of(piece * rows_at_once, rows_at_once), rows_at_once)], 0.0)
        return (total * scale).astype(BF16)

    def pack_time(piece, carry):
        for k in range(TB):
            part = gathered(acc_t, time_of, k, piece).reshape(-1, NC, ROWS, TILE)
            pt[pl.ds(k * (per_x // NC) + piece * part.shape[0], part.shape[0])] = part
        return carry

    lax.fori_loop(0, TILE // rows_at_once, pack_time, 0)
    for n, (i, j) in enumerate(NEAR):
        row, core = near(i, j)
        send(pt.at[pl.ds(row, NH), core], rx.at[n], t_x, n, at_near(i, j))

    def pack_series(piece, carry):
        per = NY * ROWS // rows_at_once
        for k in range(SB):
            part = gathered(acc_s, series_of, k, piece).reshape(-1, ROWS, TILE)
            there = (k * per_z + piece // per, pl.ds(piece % per * part.shape[0], part.shape[0]))
            pa[there] = part[..., :HALF]
            pb[there] = part[..., HALF:]
        return carry

    lax.fori_loop(0, TILE // rows_at_once, pack_series, 0)
    for d in range(1, NZ):
        there = (z + d) % NZ
        send(pa.at[there], za.at[d - 1], sa_z, d - 1, at_z(there))
    for d in range(1, NY):
        there = (y + d) % NY
        send(pb.at[:, there], yb.at[d - 1], sb_y, d - 1, at_y(there))

    def widen(rows, first):
        rows = rows.astype(F32).reshape(-1, TILE)
        wf[0, pl.ds(first * ROWS, rows.shape[0])] = rows[:, :HALF]
        wf[1, pl.ds(first * ROWS, rows.shape[0])] = rows[:, HALF:]

    nothing = jnp.zeros((HALO // NC, NC, ROWS, TILE), BF16)
    widen(xw[...], HALO)

    @pl.when(takes_past)
    def _():
        take_past.wait_recv()
        widen(before[...], 0)

    @pl.when(jnp.logical_not(takes_past))
    def _():
        widen(nothing, 0)

    @pl.when(takes_next)
    def _():
        take_next.wait_recv()
        widen(after[...], HALO + SLAB)

    @pl.when(jnp.logical_not(takes_next))
    def _():
        widen(nothing, HALO + SLAB)

    steps = tm * (SLAB * ROWS) + s * ROWS + lax.broadcasted_iota(jnp.int32, (ERR, HALF), 0)
    inside = (steps >= LMAX) & (steps < NZ * NY * SLAB * ROWS)

    base = (HALO + s) * ROWS

    def errors(side):
        def add(m, total):
            w = ww[side, pl.ds(m, 1), :]
            return total + w * wf[side, pl.ds(base - lags[m], ERR), :]

        pred = lax.fori_loop(0, lags.shape[0], add, jnp.zeros((ERR, HALF), F32))
        eb[side] = jnp.where(inside, wf[side, pl.ds(pl.multiple_of(base, ROWS), ERR), :] - pred, 0.0)

    def ahead(side):
        def add(m, total):
            w = ww[side, pl.ds(m, 1), :]
            return total + w * eb[side, pl.ds(lags[m], ROWS), :]

        return lax.fori_loop(0, lags.shape[0], add, jnp.zeros((ROWS, HALF), F32))

    errors(0)

    for n, (i, j) in enumerate(NEAR):
        arrive(rx.at[n], t_x, n, at_near(i, j))
    total = pt[pl.ds(x * NH, NH), c].astype(F32)
    for n in range(len(NEAR)):
        total = total + rx[n].astype(F32)
    qx[...] = total
    send(qx.at[1 - h], rh, t_h, 0, (tm, s_far))

    for d in range(1, NY):
        arrive(yb.at[d - 1], sb_y, d - 1, at_y((y + d) % NY))
    total = pb[:, y].astype(F32)
    for d in range(1, NY):
        total = total + yb[d - 1].astype(F32)
    qb[...] = total
    for d in range(1, NZ):
        there = (z + d) % NZ
        send(qb.at[there], zb.at[d - 1], sb_z, d - 1, at_z(there))
    for d in range(1, NZ):
        arrive(za.at[d - 1], sa_z, d - 1, at_z((z + d) % NZ))
    total = pa[z].astype(F32)
    for d in range(1, NZ):
        total = total + za[d - 1].astype(F32)
    qa[...] = total
    for d in range(1, NY):
        there = (y + d) % NY
        send(qa.at[there], ya.at[d - 1], sa_y, d - 1, at_y(there))

    errors(1)
    grads = [2.0 * (eb[side, pl.ds(0, ROWS), :] - ahead(side)) for side in range(2)]
    arrive(rh, t_h, 0, (tm, s_far))
    own = qx[h] + rh[...]
    out[1] = own + jnp.concatenate(grads, axis=1)

    for d in range(1, NZ):
        arrive(zb.at[d - 1], sb_z, d - 1, at_z((z + d) % NZ))
    right = qb[z]
    for d in range(1, NZ):
        right = right + zb[d - 1]
    for d in range(1, NY):
        arrive(ya.at[d - 1], sa_y, d - 1, at_y((y + d) % NY))
    left = qa[y]
    for d in range(1, NY):
        left = left + ya[d - 1]
    out[0] = jnp.concatenate([left, right], axis=1)

    for one in sent:
        one.wait_send()

    @pl.when(gives_past)
    def _():
        give_past.wait_send()

    @pl.when(gives_next)
    def _():
        give_next.wait_send()


def shards(series_factors, time_factors, tile_values, tile_blocks, tile_counts, lags, lag_weights):
    vmem = pl.BlockSpec(memory_space=pltpu.VMEM)
    anywhere = pl.BlockSpec(memory_space=pl.ANY)
    slots = tile_values.shape[0]
    own = jax.ShapeDtypeStruct((2, ROWS, TILE), F32)

    def pair(n):
        return pltpu.SemaphoreType.DMA((2, n))

    both = pl.pallas_call(
            kernel,
            out_shape=own,
            in_specs=[anywhere] * 7,
            out_specs=vmem,
            scratch_shapes=[
                pltpu.VMEM((ROWS, TILE), BF16),
                pltpu.VMEM((ROWS, TILE), BF16),
                pltpu.SMEM((2, slots), jnp.int32),
                pltpu.SMEM((1,), jnp.int32),
                pltpu.SMEM(lags.shape, jnp.int32),
                pltpu.VMEM(lag_weights.shape, F32),
                pltpu.VMEM((slots, TILE, TILE), BF16),
                pltpu.VMEM((NZ, NY, ROWS, HALF), BF16),
                pltpu.VMEM((NZ, NY, ROWS, HALF), BF16),
                pltpu.VMEM((SLAB // NC, NC, ROWS, TILE), BF16),
                pltpu.VMEM((HALO // NC, NC, ROWS, TILE), BF16),
                pltpu.VMEM((HALO // NC, NC, ROWS, TILE), BF16),
                pltpu.VMEM((slots, TILE, TILE), F32),
                pltpu.VMEM((slots, TILE, TILE), F32),
                pltpu.VMEM((NZ, NY, ROWS, HALF), BF16),
                pltpu.VMEM((NZ, NY, ROWS, HALF), BF16),
                pltpu.VMEM((SLAB // NC, NC, ROWS, TILE), BF16),
                pltpu.VMEM((NZ - 1, NY, ROWS, HALF), BF16),
                pltpu.VMEM((NY - 1, NZ, ROWS, HALF), BF16),
                pltpu.VMEM((NY, ROWS, HALF), F32),
                pltpu.VMEM((NZ, ROWS, HALF), F32),
                pltpu.VMEM((NY - 1, ROWS, HALF), F32),
                pltpu.VMEM((NZ - 1, ROWS, HALF), F32),
                pltpu.VMEM((len(NEAR), NH, ROWS, TILE), BF16),
                pltpu.VMEM((NH, ROWS, TILE), F32),
                pltpu.VMEM((ROWS, TILE), F32),
                pltpu.VMEM((2, (SLAB + 2 * HALO) * ROWS, HALF), F32),
                pltpu.VMEM((2, ERR, HALF), F32),
                pltpu.VMEM((2, *lags.shape, HALF), F32),
                pltpu.SemaphoreType.DMA((7,)),
                pair(NY - 1), pair(NZ - 1), pair(NZ - 1), pair(NY - 1),
                pair(1), pair(len(NEAR)), pair(2),
                pair(NZ - 1), pair(NY - 1), pair(NY - 1), pair(NZ - 1),
                pair(len(NEAR)), pair(1),
            ],
            compiler_params=pltpu.CompilerParams(
                collective_id=0, has_side_effects=True, vmem_limit_bytes=60 * 2**20
            ),
            cost_estimate=pl.CostEstimate(
                flops=slots * 6 * TILE**3, bytes_accessed=slots * 2 * TILE**2, transcendentals=0
            ),
        )(series_factors, time_factors, tile_values, tile_blocks.T, tile_counts, lags, lag_weights)
    return both[0] + 0.5 * series_factors.astype(F32), both[1] + 0.5 * time_factors.astype(F32)


def solution(mesh):
    placed = (
        P(("series", "tm"), None),
        P(("tm", "series"), None),
        P(("tm", "series"), None, None),
        P(("tm", "series"), None),
        P(("tm", "series")),
        P(),
        P(),
    )
    return jax.shard_map(
        shards,
        mesh=mesh,
        in_specs=placed,
        out_specs=(P(("series", "tm"), None), P(("tm", "series"), None)),
        check_vma=False,
    )
```

```python
import jax
import jax.numpy as jnp
from jax import lax
from jax.experimental import pallas as pl
from jax.experimental.pallas import tpu as pltpu
from jax.sharding import PartitionSpec as P

LMAX = 168
NZ, NY, NX, NH, NC = 8, 4, 4, 2, 2
ROWS = 32
TILE = 256
HALF = 128
SB = NZ * NY * ROWS // TILE
TB = NX * NH * NC * ROWS // TILE
SLAB = NX * NH * NC
SHIFTS = (2, 1, 3, 0)
NEAR = [(i, j) for i in range(NX) for j in range(NC) if i + j]
HALO = 6
ERR = ROWS + LMAX
MESH = pl.DeviceIdType.MESH
F32 = jnp.float32
BF16 = jnp.bfloat16


def contract(a, b, da, db):
    return lax.dot_general(a, b, (((da,), (db,)), ((), ())), preferred_element_type=F32)


def kernel(
    sf_in, tf_in, values, blocks_in, counts_in, lags_in, weights_in, out,
    sf, tf, blocks, counts, lags, weights, left_over, tv, fa, fb, xw, before, after, acc_s, acc_t, pa, pb, pt, za, yb, qa, qb, ya, zb, qb16,
    rx, qx, rh, wf, eb, ww, local_sem,
    fa_y, fa_z, fb_z, fb_y, x_h, x_x, halo, sa_z, sa_y, sb_y, sb_z, t_x, t_h,
):
    tm, s = lax.axis_index("tm"), lax.axis_index("series")
    z, y = tm // NY, tm % NY
    x, h, c = s // (NH * NC), s // NC % NH, s % NC
    s_far = s + NC * (1 - 2 * h)

    def at_z(i):
        return (i * NY + y, s)

    def at_y(i):
        return (z * NY + i, s)

    def near(i, j):
        return (x + i) % NX * NH, (c + j) % NC

    def at_near(i, j):
        row, core = near(i, j)
        return (tm, (row + h) * NC + core)

    def from_near(i, j):
        return near(NX - i, NC - j)

    takes_past = (s < HALO) & (tm > 0)
    gives_past = (s < HALO) & (tm < NZ * NY - 1)
    takes_next = (s >= SLAB - HALO) & (tm < NZ * NY - 1)
    gives_next = (s >= SLAB - HALO) & (tm > 0)

    barrier = pltpu.get_barrier_semaphore()

    def greet(device):
        pl.semaphore_signal(barrier, inc=1, device_id=device, device_id_type=MESH)

    for d in range(1, NY):
        greet(at_y((y + d) % NY))
    for d in range(1, NZ):
        greet(at_z((z + d) % NZ))
    for i, j in NEAR:
        greet(at_near(i, j))
    greet((tm, s_far))

    @pl.when(takes_past)
    def _():
        greet((tm - 1, s))

    @pl.when(takes_next)
    def _():
        greet((tm + 1, s))

    loads = [
        pltpu.make_async_copy(src, dst, local_sem.at[i])
        for i, (src, dst) in enumerate(
            [(tf_in, tf), (sf_in, sf), (values, tv), (weights_in, weights), (lags_in, lags), (blocks_in, blocks), (counts_in, counts)]
        )
    ]
    for one in loads:
        one.start()

    loads[0].wait()
    loads[1].wait()
    fa[z, y] = sf[:, :HALF]
    fb[z, y] = sf[:, HALF:]
    xw[x * NH + h, c] = tf[...]
    more = jnp.where(gives_past | gives_next, 1, 0)
    pl.semaphore_wait(barrier, NY - 1 + NZ - 1 + len(NEAR) + 1 + more)

    sent = []

    def copy(src, dst, sems, i, device):
        i = i if isinstance(i, tuple) else (i, i)
        return pltpu.make_async_remote_copy(
            src_ref=src, dst_ref=dst, send_sem=sems.at[0, i[0]], recv_sem=sems.at[1, i[1]],
            device_id=device, device_id_type=MESH,
        )

    def send(src, dst, sems, i, device):
        one = copy(src, dst, sems, i, device)
        one.start()
        sent.append(one)

    def arrive(dst, sems, i, device):
        copy(dst, dst, sems, i, device).wait_recv()

    send(xw.at[x * NH + h, c], xw.at[x * NH + h, c], x_h, 0, (tm, s_far))
    for d in range(1, NY):
        send(fa.at[z, y], fa.at[z, y], fa_y, d - 1, at_y((y + d) % NY))
    for d in range(1, NZ):
        send(fb.at[z, y], fb.at[z, y], fb_z, d - 1, at_z((z + d) % NZ))

    for d in range(1, NY):
        arrive(fa.at[z, (y + NY - d) % NY], fa_y, d - 1, at_y((y + d) % NY))
    for d in range(1, NZ):
        send(fa.at[z], fa.at[z], fa_z, d - 1, at_z((z + d) % NZ))
    for d in range(1, NZ):
        arrive(fb.at[(z + NZ - d) % NZ, y], fb_z, d - 1, at_z((z + d) % NZ))
    for d in range(1, NY):
        send(fb.at[:, y], fb.at[:, y], fb_y, d - 1, at_y((y + d) % NY))

    arrive(xw.at[x * NH + 1 - h, c], x_h, 0, (tm, s_far))
    part = xw.at[pl.ds(x * NH, NH), c]
    for n, (i, j) in enumerate(NEAR):
        send(part, part, x_x, n, at_near(i, j))
    for one in loads[2:]:
        one.wait()
    ww[0] = weights[:, :HALF]
    ww[1] = weights[:, HALF:]
    for n, (i, j) in enumerate(NEAR):
        row, core = from_near(i, j)
        arrive(xw.at[pl.ds(row, NH), core], x_x, n, at_near(i, j))
    give_past = copy(xw.at[pl.ds(SLAB // NC - HALO // NC, HALO // NC)], before, halo, 0, (tm + 1, s))
    give_next = copy(xw.at[pl.ds(0, HALO // NC)], after, halo, 1, (tm - 1, s))
    take_past = copy(before, before, halo, 0, (tm - 1, s))
    take_next = copy(after, after, halo, 1, (tm + 1, s))

    @pl.when(gives_past)
    def _():
        give_past.start()

    @pl.when(gives_next)
    def _():
        give_next.start()

    for d in range(1, NZ):
        arrive(fa.at[(z + NZ - d) % NZ], fa_z, d - 1, at_z((z + d) % NZ))
    for d in range(1, NY):
        arrive(fb.at[:, (y + NY - d) % NY], fb_y, d - 1, at_y((y + d) % NY))

    used = counts[0]
    per_z = TILE // (NY * ROWS)
    per_x = TILE // ROWS

    def factor_rows(at):
        left = fa[pl.ds(at * per_z, per_z)].reshape(TILE, HALF)
        right = fb[pl.ds(at * per_z, per_z)].reshape(TILE, HALF)
        return jnp.concatenate([left, right], axis=1)

    series_of, time_of = [], []
    for m in range(values.shape[0]):
        at_series = lax.rem(blocks[0, m], SB)
        at_time = lax.rem(blocks[1, m], TB)
        series_of.append(at_series)
        time_of.append(at_time)
        f = factor_rows(at_series)
        t = xw[pl.ds(at_time * (per_x // NC), per_x // NC)].reshape(TILE, TILE)
        pred = contract(f, t, 1, 1)
        resid = jnp.where(m < used, tv[m].astype(F32) - pred, 0.0).astype(BF16)
        left_over[m] = resid
        acc_s[m] = contract(resid, t, 1, 0)

    scale = -1.0 / TILE
    rows_at_once = 64

    def gathered(acc, places, k, piece):
        total = jnp.zeros((rows_at_once, TILE), F32)
        for m, place in enumerate(places):
            total = total + jnp.where(place == k, acc[m, pl.ds(pl.multiple_of(piece * rows_at_once, rows_at_once), rows_at_once)], 0.0)
        return (total * scale).astype(BF16)

    per = NY * ROWS // rows_at_once
    own_block = z // per_z

    def pack_series(k):
        def one(piece, carry):
            part = gathered(acc_s, series_of, k, piece).reshape(-1, ROWS, TILE)
            there = (k * per_z + piece // per, pl.ds(piece % per * part.shape[0], part.shape[0]))
            pa[there] = part[..., :HALF]
            pb[there] = part[..., HALF:]
            return carry

        lax.fori_loop(0, TILE // rows_at_once, one, 0)

    for n, shift in enumerate(SHIFTS):
        k = (own_block + shift) % SB
        pack_series(k)
        for e in range(per_z if shift else 1):
            there = k * per_z + e if shift else own_block * per_z + (z + 1) % per_z
            send(pa.at[there], za.at[z], sa_z, (n * per_z + e, z), at_z(there))
    for d in range(1, NY):
        there = (y + d) % NY
        send(pb.at[:, there], yb.at[d - 1], sb_y, d - 1, at_y(there))

    for m in range(values.shape[0]):
        acc_t[m] = contract(left_over[m], factor_rows(series_of[m]), 0, 0)

    def pack_time(piece, carry):
        for k in range(TB):
            part = gathered(acc_t, time_of, k, piece).reshape(-1, NC, ROWS, TILE)
            pt[pl.ds(k * (per_x // NC) + piece * part.shape[0], part.shape[0])] = part
        return carry

    lax.fori_loop(0, TILE // rows_at_once, pack_time, 0)
    for n, (i, j) in enumerate(NEAR):
        row, core = near(i, j)
        send(pt.at[pl.ds(row, NH), core], rx.at[n], t_x, n, at_near(i, j))

    def widen(rows, first):
        rows = rows.astype(F32).reshape(-1, TILE)
        wf[0, pl.ds(first * ROWS, rows.shape[0])] = rows[:, :HALF]
        wf[1, pl.ds(first * ROWS, rows.shape[0])] = rows[:, HALF:]

    nothing = jnp.zeros((HALO // NC, NC, ROWS, TILE), BF16)
    widen(xw[...], HALO)

    @pl.when(takes_past)
    def _():
        take_past.wait_recv()
        widen(before[...], 0)

    @pl.when(jnp.logical_not(takes_past))
    def _():
        widen(nothing, 0)

    @pl.when(takes_next)
    def _():
        take_next.wait_recv()
        widen(after[...], HALO + SLAB)

    @pl.when(jnp.logical_not(takes_next))
    def _():
        widen(nothing, HALO + SLAB)

    steps = tm * (SLAB * ROWS) + s * ROWS + lax.broadcasted_iota(jnp.int32, (ERR, HALF), 0)
    inside = (steps >= LMAX) & (steps < NZ * NY * SLAB * ROWS)

    base = (HALO + s) * ROWS

    def errors(side):
        def add(m, total):
            w = ww[side, pl.ds(m, 1), :]
            return total + w * wf[side, pl.ds(base - lags[m], ERR), :]

        pred = lax.fori_loop(0, lags.shape[0], add, jnp.zeros((ERR, HALF), F32))
        eb[side] = jnp.where(inside, wf[side, pl.ds(pl.multiple_of(base, ROWS), ERR), :] - pred, 0.0)

    def ahead(side):
        def add(m, total):
            w = ww[side, pl.ds(m, 1), :]
            return total + w * eb[side, pl.ds(lags[m], ROWS), :]

        return lax.fori_loop(0, lags.shape[0], add, jnp.zeros((ROWS, HALF), F32))

    errors(0)

    for n, (i, j) in enumerate(NEAR):
        arrive(rx.at[n], t_x, n, at_near(i, j))
    total = pt[pl.ds(x * NH, NH), c].astype(F32)
    for n in range(len(NEAR)):
        total = total + rx[n].astype(F32)
    qx[...] = total
    send(qx.at[1 - h], rh, t_h, 0, (tm, s_far))

    for d in range(1, NY):
        arrive(yb.at[d - 1], sb_y, d - 1, at_y((y + d) % NY))
    total = pb[:, y].astype(F32)
    for d in range(1, NY):
        total = total + yb[d - 1].astype(F32)
    qb[...] = total
    qb16[...] = total.astype(BF16)
    for d in range(1, NZ):
        there = (z + d) % NZ
        send(qb16.at[there], zb.at[d - 1], sb_z, d - 1, at_z(there))
    for n, shift in enumerate(SHIFTS):
        for e in range(per_z if shift else 1):
            source = (own_block + SB - shift) % SB * per_z + e if shift else own_block * per_z + (z + 1) % per_z
            arrive(za.at[source], sa_z, (0, source), at_z(source))
    total = pa[z].astype(F32)
    for d in range(1, NZ):
        total = total + za[(z + d) % NZ].astype(F32)
    qa[...] = total
    for d in range(1, NY):
        there = (y + d) % NY
        send(qa.at[there], ya.at[d - 1], sa_y, d - 1, at_y(there))

    errors(1)
    grads = [2.0 * (eb[side, pl.ds(0, ROWS), :] - ahead(side)) for side in range(2)]
    arrive(rh, t_h, 0, (tm, s_far))
    own = qx[h] + rh[...]
    out[1] = own + jnp.concatenate(grads, axis=1)

    for d in range(1, NZ):
        arrive(zb.at[d - 1], sb_z, d - 1, at_z((z + d) % NZ))
    right = qb[z]
    for d in range(1, NZ):
        right = right + zb[d - 1].astype(F32)
    for d in range(1, NY):
        arrive(ya.at[d - 1], sa_y, d - 1, at_y((y + d) % NY))
    left = qa[y]
    for d in range(1, NY):
        left = left + ya[d - 1]
    out[0] = jnp.concatenate([left, right], axis=1)

    for one in sent:
        one.wait_send()

    @pl.when(gives_past)
    def _():
        give_past.wait_send()

    @pl.when(gives_next)
    def _():
        give_next.wait_send()


def shards(series_factors, time_factors, tile_values, tile_blocks, tile_counts, lags, lag_weights):
    vmem = pl.BlockSpec(memory_space=pltpu.VMEM)
    anywhere = pl.BlockSpec(memory_space=pl.ANY)
    slots = tile_values.shape[0]
    own = jax.ShapeDtypeStruct((2, ROWS, TILE), F32)

    def pair(n):
        return pltpu.SemaphoreType.DMA((2, n))

    both = pl.pallas_call(
            kernel,
            out_shape=own,
            in_specs=[anywhere] * 7,
            out_specs=vmem,
            scratch_shapes=[
                pltpu.VMEM((ROWS, TILE), BF16),
                pltpu.VMEM((ROWS, TILE), BF16),
                pltpu.SMEM((2, slots), jnp.int32),
                pltpu.SMEM((1,), jnp.int32),
                pltpu.SMEM(lags.shape, jnp.int32),
                pltpu.VMEM(lag_weights.shape, F32),
                pltpu.VMEM((slots, TILE, TILE), BF16),
                pltpu.VMEM((slots, TILE, TILE), BF16),
                pltpu.VMEM((NZ, NY, ROWS, HALF), BF16),
                pltpu.VMEM((NZ, NY, ROWS, HALF), BF16),
                pltpu.VMEM((SLAB // NC, NC, ROWS, TILE), BF16),
                pltpu.VMEM((HALO // NC, NC, ROWS, TILE), BF16),
                pltpu.VMEM((HALO // NC, NC, ROWS, TILE), BF16),
                pltpu.VMEM((slots, TILE, TILE), F32),
                pltpu.VMEM((slots, TILE, TILE), F32),
                pltpu.VMEM((NZ, NY, ROWS, HALF), BF16),
                pltpu.VMEM((NZ, NY, ROWS, HALF), BF16),
                pltpu.VMEM((SLAB // NC, NC, ROWS, TILE), BF16),
                pltpu.VMEM((NZ, NY, ROWS, HALF), BF16),
                pltpu.VMEM((NY - 1, NZ, ROWS, HALF), BF16),
                pltpu.VMEM((NY, ROWS, HALF), F32),
                pltpu.VMEM((NZ, ROWS, HALF), F32),
                pltpu.VMEM((NY - 1, ROWS, HALF), F32),
                pltpu.VMEM((NZ - 1, ROWS, HALF), BF16),
                pltpu.VMEM((NZ, ROWS, HALF), BF16),
                pltpu.VMEM((len(NEAR), NH, ROWS, TILE), BF16),
                pltpu.VMEM((NH, ROWS, TILE), F32),
                pltpu.VMEM((ROWS, TILE), F32),
                pltpu.VMEM((2, (SLAB + 2 * HALO) * ROWS, HALF), F32),
                pltpu.VMEM((2, ERR, HALF), F32),
                pltpu.VMEM((2, *lags.shape, HALF), F32),
                pltpu.SemaphoreType.DMA((7,)),
                pair(NY - 1), pair(NZ - 1), pair(NZ - 1), pair(NY - 1),
                pair(1), pair(len(NEAR)), pair(2),
                pair(NZ), pair(NY - 1), pair((NY - 1) * SB), pair(NZ - 1),
                pair(len(NEAR)), pair(1),
            ],
            compiler_params=pltpu.CompilerParams(
                collective_id=0, has_side_effects=True, vmem_limit_bytes=60 * 2**20
            ),
            cost_estimate=pl.CostEstimate(
                flops=slots * 6 * TILE**3, bytes_accessed=slots * 2 * TILE**2, transcendentals=0
            ),
        )(series_factors, time_factors, tile_values, tile_blocks.T, tile_counts, lags, lag_weights)
    return both[0] + 0.5 * series_factors.astype(F32), both[1] + 0.5 * time_factors.astype(F32)


def solution(mesh):
    placed = (
        P(("series", "tm"), None),
        P(("tm", "series"), None),
        P(("tm", "series"), None, None),
        P(("tm", "series"), None),
        P(("tm", "series")),
        P(),
        P(),
    )
    return jax.shard_map(
        shards,
        mesh=mesh,
        in_specs=placed,
        out_specs=(P(("series", "tm"), None), P(("tm", "series"), None)),
        check_vma=False,
    )
```

```python
import jax
import jax.numpy as jnp
from jax import lax
from jax.experimental import pallas as pl
from jax.experimental.pallas import tpu as pltpu
from jax.sharding import PartitionSpec as P

LMAX = 168
NZ, NY, NX, NH, NC = 8, 4, 4, 2, 2
ROWS = 32
TILE = 256
HALF = 128
SB = NZ * NY * ROWS // TILE
TB = NX * NH * NC * ROWS // TILE
SLAB = NX * NH * NC
SHIFTS = (2, 1, 3, 0)
NEAR = [(i, j) for i in range(NX) for j in range(NC) if i + j]
HALO = 6
ERR = ROWS + LMAX
MESH = pl.DeviceIdType.MESH
F32 = jnp.float32
BF16 = jnp.bfloat16


def contract(a, b, da, db):
    return lax.dot_general(a, b, (((da,), (db,)), ((), ())), preferred_element_type=F32)


def kernel(
    sf_in, tf_in, values, blocks_in, counts_in, lags_in, weights_in, out,
    sf, tf, blocks, counts, lags, weights, left_over, tv, fa, fb, xw, before, after, acc_s, acc_t, pa, pb, pt, za, yb, qa, qb, ya, zb, qb16,
    rx, qx, rh, wf, eb, ww, local_sem,
    fa_y, fa_z, fb_z, fb_y, x_h, x_x, halo, sa_z, sa_y, sb_y, sb_z, t_x, t_h,
):
    tm, s = lax.axis_index("tm"), lax.axis_index("series")
    z, y = tm // NY, tm % NY
    x, h, c = s // (NH * NC), s // NC % NH, s % NC
    s_far = s + NC * (1 - 2 * h)

    def at_z(i):
        return (i * NY + y, s)

    def at_y(i):
        return (z * NY + i, s)

    def near(i, j):
        return (x + i) % NX * NH, (c + j) % NC

    def at_near(i, j):
        row, core = near(i, j)
        return (tm, (row + h) * NC + core)

    def from_near(i, j):
        return near(NX - i, NC - j)

    takes_past = (s < HALO) & (tm > 0)
    gives_past = (s < HALO) & (tm < NZ * NY - 1)
    takes_next = (s >= SLAB - HALO) & (tm < NZ * NY - 1)
    gives_next = (s >= SLAB - HALO) & (tm > 0)

    barrier = pltpu.get_barrier_semaphore()

    def greet(device):
        pl.semaphore_signal(barrier, inc=1, device_id=device, device_id_type=MESH)

    for d in range(1, NY):
        greet(at_y((y + d) % NY))
    for d in range(1, NZ):
        greet(at_z((z + d) % NZ))
    for i, j in NEAR:
        greet(at_near(i, j))
    greet((tm, s_far))

    @pl.when(takes_past)
    def _():
        greet((tm - 1, s))

    @pl.when(takes_next)
    def _():
        greet((tm + 1, s))

    loads = [
        pltpu.make_async_copy(src, dst, local_sem.at[i])
        for i, (src, dst) in enumerate(
            [(tf_in, tf), (sf_in, sf), (values, tv), (weights_in, weights), (lags_in, lags), (blocks_in, blocks), (counts_in, counts)]
        )
    ]
    for one in loads:
        one.start()

    loads[0].wait()
    loads[1].wait()
    fa[z, y] = sf[:, :HALF]
    fb[z, y] = sf[:, HALF:]
    xw[x * NH + h, c] = tf[...]
    more = jnp.where(gives_past | gives_next, 1, 0)
    pl.semaphore_wait(barrier, NY - 1 + NZ - 1 + len(NEAR) + 1 + more)

    sent = []

    def copy(src, dst, sems, i, device):
        i = i if isinstance(i, tuple) else (i, i)
        return pltpu.make_async_remote_copy(
            src_ref=src, dst_ref=dst, send_sem=sems.at[0, i[0]], recv_sem=sems.at[1, i[1]],
            device_id=device, device_id_type=MESH,
        )

    def send(src, dst, sems, i, device):
        one = copy(src, dst, sems, i, device)
        one.start()
        sent.append(one)

    def arrive(dst, sems, i, device):
        copy(dst, dst, sems, i, device).wait_recv()

    send(xw.at[x * NH + h, c], xw.at[x * NH + h, c], x_h, 0, (tm, s_far))
    for d in range(1, NY):
        send(fa.at[z, y], fa.at[z, y], fa_y, d - 1, at_y((y + d) % NY))
    for d in range(1, NZ):
        send(fb.at[z, y], fb.at[z, y], fb_z, d - 1, at_z((z + d) % NZ))

    for d in range(1, NY):
        arrive(fa.at[z, (y + NY - d) % NY], fa_y, d - 1, at_y((y + d) % NY))
    for d in range(1, NZ):
        send(fa.at[z], fa.at[z], fa_z, d - 1, at_z((z + d) % NZ))
    for d in range(1, NZ):
        arrive(fb.at[(z + NZ - d) % NZ, y], fb_z, d - 1, at_z((z + d) % NZ))
    for d in range(1, NY):
        send(fb.at[:, y], fb.at[:, y], fb_y, d - 1, at_y((y + d) % NY))

    arrive(xw.at[x * NH + 1 - h, c], x_h, 0, (tm, s_far))
    part = xw.at[pl.ds(x * NH, NH), c]
    for n, (i, j) in enumerate(NEAR):
        send(part, part, x_x, n, at_near(i, j))
    for one in loads[2:]:
        one.wait()
    ww[0] = weights[:, :HALF]
    ww[1] = weights[:, HALF:]
    for n, (i, j) in enumerate(NEAR):
        row, core = from_near(i, j)
        arrive(xw.at[pl.ds(row, NH), core], x_x, n, at_near(i, j))
    give_past = copy(xw.at[pl.ds(SLAB // NC - HALO // NC, HALO // NC)], before, halo, 0, (tm + 1, s))
    give_next = copy(xw.at[pl.ds(0, HALO // NC)], after, halo, 1, (tm - 1, s))
    take_past = copy(before, before, halo, 0, (tm - 1, s))
    take_next = copy(after, after, halo, 1, (tm + 1, s))

    @pl.when(gives_past)
    def _():
        give_past.start()

    @pl.when(gives_next)
    def _():
        give_next.start()

    for d in range(1, NZ):
        arrive(fa.at[(z + NZ - d) % NZ], fa_z, d - 1, at_z((z + d) % NZ))
    for d in range(1, NY):
        arrive(fb.at[:, (y + NY - d) % NY], fb_y, d - 1, at_y((y + d) % NY))

    gathers = list(sent)
    sent.clear()
    used = counts[0]
    per_z = TILE // (NY * ROWS)
    per_x = TILE // ROWS

    def factor_rows(at):
        left = fa[pl.ds(at * per_z, per_z)].reshape(TILE, HALF)
        right = fb[pl.ds(at * per_z, per_z)].reshape(TILE, HALF)
        return jnp.concatenate([left, right], axis=1)

    series_of, time_of = [], []
    for m in range(values.shape[0]):
        at_series = lax.rem(blocks[0, m], SB)
        at_time = lax.rem(blocks[1, m], TB)
        series_of.append(at_series)
        time_of.append(at_time)
        f = factor_rows(at_series)
        t = xw[pl.ds(at_time * (per_x // NC), per_x // NC)].reshape(TILE, TILE)
        pred = contract(f, t, 1, 1)
        resid = jnp.where(m < used, tv[m].astype(F32) - pred, 0.0).astype(BF16)
        left_over[m] = resid
        acc_s[m] = contract(resid, t, 1, 0)

    scale = -1.0 / TILE
    rows_at_once = 64

    def gathered(acc, places, k, piece):
        total = jnp.zeros((rows_at_once, TILE), F32)
        for m, place in enumerate(places):
            total = total + jnp.where(place == k, acc[m, pl.ds(pl.multiple_of(piece * rows_at_once, rows_at_once), rows_at_once)], 0.0)
        return (total * scale).astype(BF16)

    per = NY * ROWS // rows_at_once
    own_block = z // per_z

    def pack_series(k):
        def one(piece, carry):
            part = gathered(acc_s, series_of, k, piece).reshape(-1, ROWS, TILE)
            there = (k * per_z + piece // per, pl.ds(piece % per * part.shape[0], part.shape[0]))
            pa[there] = part[..., :HALF]
            pb[there] = part[..., HALF:]
            return carry

        lax.fori_loop(0, TILE // rows_at_once, one, 0)

    for n, shift in enumerate(SHIFTS):
        k = (own_block + shift) % SB
        pack_series(k)
        for e in range(per_z if shift else 1):
            there = k * per_z + e if shift else own_block * per_z + (z + 1) % per_z
            send(pa.at[there], za.at[z], sa_z, (n * per_z + e, z), at_z(there))
    for d in (2, 1, 3):
        there = (y + d) % NY
        send(pb.at[:, there], yb.at[d - 1], sb_y, d - 1, at_y(there))

    for m in range(values.shape[0]):
        acc_t[m] = contract(left_over[m], factor_rows(series_of[m]), 0, 0)

    def pack_time(piece, carry):
        for k in range(TB):
            part = gathered(acc_t, time_of, k, piece).reshape(-1, NC, ROWS, TILE)
            pt[pl.ds(k * (per_x // NC) + piece * part.shape[0], part.shape[0])] = part
        return carry

    lax.fori_loop(0, TILE // rows_at_once, pack_time, 0)
    for n, (i, j) in enumerate(NEAR):
        row, core = near(i, j)
        send(pt.at[pl.ds(row, NH), core], rx.at[n], t_x, n, at_near(i, j))

    def widen(rows, first):
        rows = rows.astype(F32).reshape(-1, TILE)
        wf[0, pl.ds(first * ROWS, rows.shape[0])] = rows[:, :HALF]
        wf[1, pl.ds(first * ROWS, rows.shape[0])] = rows[:, HALF:]

    nothing = jnp.zeros((HALO // NC, NC, ROWS, TILE), BF16)
    widen(xw[...], HALO)

    @pl.when(takes_past)
    def _():
        take_past.wait_recv()
        widen(before[...], 0)

    @pl.when(jnp.logical_not(takes_past))
    def _():
        widen(nothing, 0)

    @pl.when(takes_next)
    def _():
        take_next.wait_recv()
        widen(after[...], HALO + SLAB)

    @pl.when(jnp.logical_not(takes_next))
    def _():
        widen(nothing, HALO + SLAB)

    steps = tm * (SLAB * ROWS) + s * ROWS + lax.broadcasted_iota(jnp.int32, (ERR, HALF), 0)
    inside = (steps >= LMAX) & (steps < NZ * NY * SLAB * ROWS)

    base = (HALO + s) * ROWS

    def errors(side):
        def add(m, total):
            w = ww[side, pl.ds(m, 1), :]
            return total + w * wf[side, pl.ds(base - lags[m], ERR), :]

        pred = lax.fori_loop(0, lags.shape[0], add, jnp.zeros((ERR, HALF), F32))
        eb[side] = jnp.where(inside, wf[side, pl.ds(pl.multiple_of(base, ROWS), ERR), :] - pred, 0.0)

    def ahead(side):
        def add(m, total):
            w = ww[side, pl.ds(m, 1), :]
            return total + w * eb[side, pl.ds(lags[m], ROWS), :]

        return lax.fori_loop(0, lags.shape[0], add, jnp.zeros((ROWS, HALF), F32))

    errors(0)

    for one in gathers:
        one.wait_send()
    for n, (i, j) in enumerate(NEAR):
        arrive(rx.at[n], t_x, n, at_near(i, j))
    total = pt[pl.ds(x * NH, NH), c].astype(F32)
    for n in range(len(NEAR)):
        total = total + rx[n].astype(F32)
    qx[...] = total
    send(qx.at[1 - h], rh, t_h, 0, (tm, s_far))

    for d in range(1, NY):
        arrive(yb.at[d - 1], sb_y, d - 1, at_y((y + d) % NY))
    total = pb[:, y].astype(F32)
    for d in range(1, NY):
        total = total + yb[d - 1].astype(F32)
    qb[...] = total
    qb16[...] = total.astype(BF16)
    for d in range(1, NZ):
        there = (z + d) % NZ
        send(qb16.at[there], zb.at[d - 1], sb_z, d - 1, at_z(there))
    for n, shift in enumerate(SHIFTS):
        for e in range(per_z if shift else 1):
            source = (own_block + SB - shift) % SB * per_z + e if shift else own_block * per_z + (z + 1) % per_z
            arrive(za.at[source], sa_z, (0, source), at_z(source))
    total = pa[z].astype(F32)
    for d in range(1, NZ):
        total = total + za[(z + d) % NZ].astype(F32)
    qa[...] = total
    for d in range(1, NY):
        there = (y + d) % NY
        send(qa.at[there], ya.at[d - 1], sa_y, d - 1, at_y(there))

    errors(1)
    grads = [2.0 * (eb[side, pl.ds(0, ROWS), :] - ahead(side)) for side in range(2)]
    arrive(rh, t_h, 0, (tm, s_far))
    own = qx[h] + rh[...]
    out[1] = own + jnp.concatenate(grads, axis=1)

    for d in range(1, NZ):
        arrive(zb.at[d - 1], sb_z, d - 1, at_z((z + d) % NZ))
    right = qb[z]
    for d in range(1, NZ):
        right = right + zb[d - 1].astype(F32)
    for d in range(1, NY):
        arrive(ya.at[d - 1], sa_y, d - 1, at_y((y + d) % NY))
    left = qa[y]
    for d in range(1, NY):
        left = left + ya[d - 1]
    out[0] = jnp.concatenate([left, right], axis=1)

    for one in sent:
        one.wait_send()

    @pl.when(gives_past)
    def _():
        give_past.wait_send()

    @pl.when(gives_next)
    def _():
        give_next.wait_send()


def shards(series_factors, time_factors, tile_values, tile_blocks, tile_counts, lags, lag_weights):
    vmem = pl.BlockSpec(memory_space=pltpu.VMEM)
    anywhere = pl.BlockSpec(memory_space=pl.ANY)
    slots = tile_values.shape[0]
    own = jax.ShapeDtypeStruct((2, ROWS, TILE), F32)

    def pair(n):
        return pltpu.SemaphoreType.DMA((2, n))

    both = pl.pallas_call(
            kernel,
            out_shape=own,
            in_specs=[anywhere] * 7,
            out_specs=vmem,
            scratch_shapes=[
                pltpu.VMEM((ROWS, TILE), BF16),
                pltpu.VMEM((ROWS, TILE), BF16),
                pltpu.SMEM((2, slots), jnp.int32),
                pltpu.SMEM((1,), jnp.int32),
                pltpu.SMEM(lags.shape, jnp.int32),
                pltpu.VMEM(lag_weights.shape, F32),
                pltpu.VMEM((slots, TILE, TILE), BF16),
                pltpu.VMEM((slots, TILE, TILE), BF16),
                pltpu.VMEM((NZ, NY, ROWS, HALF), BF16),
                pltpu.VMEM((NZ, NY, ROWS, HALF), BF16),
                pltpu.VMEM((SLAB // NC, NC, ROWS, TILE), BF16),
                pltpu.VMEM((HALO // NC, NC, ROWS, TILE), BF16),
                pltpu.VMEM((HALO // NC, NC, ROWS, TILE), BF16),
                pltpu.VMEM((slots, TILE, TILE), F32),
                pltpu.VMEM((slots, TILE, TILE), F32),
                pltpu.VMEM((NZ, NY, ROWS, HALF), BF16),
                pltpu.VMEM((NZ, NY, ROWS, HALF), BF16),
                pltpu.VMEM((SLAB // NC, NC, ROWS, TILE), BF16),
                pltpu.VMEM((NZ, NY, ROWS, HALF), BF16),
                pltpu.VMEM((NY - 1, NZ, ROWS, HALF), BF16),
                pltpu.VMEM((NY, ROWS, HALF), F32),
                pltpu.VMEM((NZ, ROWS, HALF), F32),
                pltpu.VMEM((NY - 1, ROWS, HALF), F32),
                pltpu.VMEM((NZ - 1, ROWS, HALF), BF16),
                pltpu.VMEM((NZ, ROWS, HALF), BF16),
                pltpu.VMEM((len(NEAR), NH, ROWS, TILE), BF16),
                pltpu.VMEM((NH, ROWS, TILE), F32),
                pltpu.VMEM((ROWS, TILE), F32),
                pltpu.VMEM((2, (SLAB + 2 * HALO) * ROWS, HALF), F32),
                pltpu.VMEM((2, ERR, HALF), F32),
                pltpu.VMEM((2, *lags.shape, HALF), F32),
                pltpu.SemaphoreType.DMA((7,)),
                pair(NY - 1), pair(NZ - 1), pair(NZ - 1), pair(NY - 1),
                pair(1), pair(len(NEAR)), pair(2),
                pair(NZ), pair(NY - 1), pair((NY - 1) * SB), pair(NZ - 1),
                pair(len(NEAR)), pair(1),
            ],
            compiler_params=pltpu.CompilerParams(
                collective_id=0, has_side_effects=True, vmem_limit_bytes=60 * 2**20
            ),
            cost_estimate=pl.CostEstimate(
                flops=slots * 6 * TILE**3, bytes_accessed=slots * 2 * TILE**2, transcendentals=0
            ),
        )(series_factors, time_factors, tile_values, tile_blocks.T, tile_counts, lags, lag_weights)
    return both[0] + 0.5 * series_factors.astype(F32), both[1] + 0.5 * time_factors.astype(F32)


def solution(mesh):
    placed = (
        P(("series", "tm"), None),
        P(("tm", "series"), None),
        P(("tm", "series"), None, None),
        P(("tm", "series"), None),
        P(("tm", "series")),
        P(),
        P(),
    )
    return jax.shard_map(
        shards,
        mesh=mesh,
        in_specs=placed,
        out_specs=(P(("series", "tm"), None), P(("tm", "series"), None)),
        check_vma=False,
    )
```

```python
import jax
import jax.numpy as jnp
from jax import lax
from jax.experimental import pallas as pl
from jax.experimental.pallas import tpu as pltpu
from jax.sharding import PartitionSpec as P

LMAX = 168
NZ, NY, NX, NH, NC = 8, 4, 4, 2, 2
ROWS = 32
TILE = 256
HALF = 128
SB = NZ * NY * ROWS // TILE
TB = NX * NH * NC * ROWS // TILE
SLAB = NX * NH * NC
SHIFTS = (2, 1, 3, 0)
NEAR = [(i, j) for i in range(NX) for j in range(NC) if i + j]
HALO = 6
ERR = ROWS + LMAX
MESH = pl.DeviceIdType.MESH
F32 = jnp.float32
BF16 = jnp.bfloat16


def contract(a, b, da, db):
    return lax.dot_general(a, b, (((da,), (db,)), ((), ())), preferred_element_type=F32)


def kernel(
    sf_in, tf_in, values, blocks_in, counts_in, lags_in, weights_in, out,
    sf, tf, blocks, counts, lags, weights, left_over, tv, fa, fb, xw, before, after, acc_s, acc_t, pa, pb, pt, za, yb, qa, qb, ya, zb, qb16,
    rx, qx, rh, wf, eb, ww, local_sem,
    fa_y, fa_z, fb_z, fb_y, x_h, x_x, halo, sa_z, sa_y, sb_y, sb_z, t_x, t_h,
):
    tm, s = lax.axis_index("tm"), lax.axis_index("series")
    z, y = tm // NY, tm % NY
    x, h, c = s // (NH * NC), s // NC % NH, s % NC
    s_far = s + NC * (1 - 2 * h)

    def at_z(i):
        return (i * NY + y, s)

    def at_y(i):
        return (z * NY + i, s)

    def near(i, j):
        return (x + i) % NX * NH, (c + j) % NC

    def at_near(i, j):
        row, core = near(i, j)
        return (tm, (row + h) * NC + core)

    def from_near(i, j):
        return near(NX - i, NC - j)

    takes_past = (s < HALO) & (tm > 0)
    gives_past = (s < HALO) & (tm < NZ * NY - 1)
    takes_next = (s >= SLAB - HALO) & (tm < NZ * NY - 1)
    gives_next = (s >= SLAB - HALO) & (tm > 0)

    barrier = pltpu.get_barrier_semaphore()

    def greet(device):
        pl.semaphore_signal(barrier, inc=1, device_id=device, device_id_type=MESH)

    for d in range(1, NY):
        greet(at_y((y + d) % NY))
    for d in range(1, NZ):
        greet(at_z((z + d) % NZ))
    for i, j in NEAR:
        greet(at_near(i, j))
    greet((tm, s_far))

    @pl.when(takes_past)
    def _():
        greet((tm - 1, s))

    @pl.when(takes_next)
    def _():
        greet((tm + 1, s))

    loads = [
        pltpu.make_async_copy(src, dst, local_sem.at[i])
        for i, (src, dst) in enumerate(
            [(tf_in, tf), (sf_in, sf), (values, tv), (weights_in, weights), (lags_in, lags), (blocks_in, blocks), (counts_in, counts)]
        )
    ]
    for one in loads:
        one.start()

    loads[0].wait()
    loads[1].wait()
    fa[z, y] = sf[:, :HALF]
    fb[z, y] = sf[:, HALF:]
    xw[x * NH + h, c] = tf[...]
    more = jnp.where(gives_past | gives_next, 1, 0)
    pl.semaphore_wait(barrier, NY - 1 + NZ - 1 + len(NEAR) + 1 + more)

    sent = []

    def copy(src, dst, sems, i, device):
        i = i if isinstance(i, tuple) else (i, i)
        return pltpu.make_async_remote_copy(
            src_ref=src, dst_ref=dst, send_sem=sems.at[0, i[0]], recv_sem=sems.at[1, i[1]],
            device_id=device, device_id_type=MESH,
        )

    def send(src, dst, sems, i, device):
        one = copy(src, dst, sems, i, device)
        one.start()
        sent.append(one)

    def arrive(dst, sems, i, device):
        copy(dst, dst, sems, i, device).wait_recv()

    send(xw.at[x * NH + h, c], xw.at[x * NH + h, c], x_h, 0, (tm, s_far))
    for d in range(1, NY):
        send(fa.at[z, y], fa.at[z, y], fa_y, d - 1, at_y((y + d) % NY))
    for d in range(1, NZ):
        send(fb.at[z, y], fb.at[z, y], fb_z, d - 1, at_z((z + d) % NZ))

    for d in range(1, NY):
        arrive(fa.at[z, (y + NY - d) % NY], fa_y, d - 1, at_y((y + d) % NY))
    for d in range(1, NZ):
        send(fa.at[z], fa.at[z], fa_z, d - 1, at_z((z + d) % NZ))
    for d in range(1, NZ):
        arrive(fb.at[(z + NZ - d) % NZ, y], fb_z, d - 1, at_z((z + d) % NZ))
    for d in range(1, NY):
        send(fb.at[:, y], fb.at[:, y], fb_y, d - 1, at_y((y + d) % NY))

    arrive(xw.at[x * NH + 1 - h, c], x_h, 0, (tm, s_far))
    part = xw.at[pl.ds(x * NH, NH), c]
    for n, (i, j) in enumerate(NEAR):
        send(part, part, x_x, n, at_near(i, j))
    for one in loads[2:]:
        one.wait()
    ww[0] = weights[:, :HALF]
    ww[1] = weights[:, HALF:]
    for n, (i, j) in enumerate(NEAR):
        row, core = from_near(i, j)
        arrive(xw.at[pl.ds(row, NH), core], x_x, n, at_near(i, j))
    give_past = copy(xw.at[pl.ds(SLAB // NC - HALO // NC, HALO // NC)], before, halo, 0, (tm + 1, s))
    give_next = copy(xw.at[pl.ds(0, HALO // NC)], after, halo, 1, (tm - 1, s))
    take_past = copy(before, before, halo, 0, (tm - 1, s))
    take_next = copy(after, after, halo, 1, (tm + 1, s))

    @pl.when(gives_past)
    def _():
        give_past.start()

    @pl.when(gives_next)
    def _():
        give_next.start()

    for d in range(1, NZ):
        arrive(fa.at[(z + NZ - d) % NZ], fa_z, d - 1, at_z((z + d) % NZ))
    for d in range(1, NY):
        arrive(fb.at[:, (y + NY - d) % NY], fb_y, d - 1, at_y((y + d) % NY))

    used = counts[0]
    per_z = TILE // (NY * ROWS)
    per_x = TILE // ROWS

    def factor_rows(at):
        left = fa[pl.ds(at * per_z, per_z)].reshape(TILE, HALF)
        right = fb[pl.ds(at * per_z, per_z)].reshape(TILE, HALF)
        return jnp.concatenate([left, right], axis=1)

    series_of, time_of = [], []
    for m in range(values.shape[0]):
        at_series = lax.rem(blocks[0, m], SB)
        at_time = lax.rem(blocks[1, m], TB)
        series_of.append(at_series)
        time_of.append(at_time)
        f = factor_rows(at_series)
        t = xw[pl.ds(at_time * (per_x // NC), per_x // NC)].reshape(TILE, TILE)
        pred = contract(f, t, 1, 1)
        resid = jnp.where(m < used, tv[m].astype(F32) - pred, 0.0).astype(BF16)
        left_over[m] = resid
        acc_s[m] = contract(resid, t, 1, 0)

    scale = -1.0 / TILE
    rows_at_once = 64

    def gathered(acc, places, k, piece):
        total = jnp.zeros((rows_at_once, TILE), F32)
        for m, place in enumerate(places):
            share = jnp.where(place == k, scale, 0.0)
            total = total + share * acc[m, pl.ds(pl.multiple_of(piece * rows_at_once, rows_at_once), rows_at_once)]
        return total.astype(BF16)

    per = NY * ROWS // rows_at_once
    own_block = z // per_z

    def pack_series(k):
        def one(piece, carry):
            part = gathered(acc_s, series_of, k, piece).reshape(-1, ROWS, TILE)
            there = (k * per_z + piece // per, pl.ds(piece % per * part.shape[0], part.shape[0]))
            pa[there] = part[..., :HALF]
            pb[there] = part[..., HALF:]
            return carry

        lax.fori_loop(0, TILE // rows_at_once, one, 0)

    for n, shift in enumerate(SHIFTS):
        k = (own_block + shift) % SB
        pack_series(k)
        for e in range(per_z if shift else 1):
            there = k * per_z + e if shift else own_block * per_z + (z + 1) % per_z
            send(pa.at[there], za.at[z], sa_z, (n * per_z + e, z), at_z(there))
    for d in range(1, NY):
        there = (y + d) % NY
        send(pb.at[:, there], yb.at[d - 1], sb_y, d - 1, at_y(there))

    for m in range(values.shape[0]):
        acc_t[m] = contract(left_over[m], factor_rows(series_of[m]), 0, 0)

    def pack_time(piece, carry):
        for k in range(TB):
            part = gathered(acc_t, time_of, k, piece).reshape(-1, NC, ROWS, TILE)
            pt[pl.ds(k * (per_x // NC) + piece * part.shape[0], part.shape[0])] = part
        return carry

    lax.fori_loop(0, TILE // rows_at_once, pack_time, 0)
    for n, (i, j) in enumerate(NEAR):
        row, core = near(i, j)
        send(pt.at[pl.ds(row, NH), core], rx.at[n], t_x, n, at_near(i, j))

    def widen(rows, first):
        rows = rows.astype(F32).reshape(-1, TILE)
        wf[0, pl.ds(first * ROWS, rows.shape[0])] = rows[:, :HALF]
        wf[1, pl.ds(first * ROWS, rows.shape[0])] = rows[:, HALF:]

    nothing = jnp.zeros((HALO // NC, NC, ROWS, TILE), BF16)
    widen(xw[...], HALO)

    @pl.when(takes_past)
    def _():
        take_past.wait_recv()
        widen(before[...], 0)

    @pl.when(jnp.logical_not(takes_past))
    def _():
        widen(nothing, 0)

    @pl.when(takes_next)
    def _():
        take_next.wait_recv()
        widen(after[...], HALO + SLAB)

    @pl.when(jnp.logical_not(takes_next))
    def _():
        widen(nothing, HALO + SLAB)

    steps = tm * (SLAB * ROWS) + s * ROWS + lax.broadcasted_iota(jnp.int32, (ERR, HALF), 0)
    inside = (steps >= LMAX) & (steps < NZ * NY * SLAB * ROWS)

    base = (HALO + s) * ROWS

    def errors(side):
        def add(m, total):
            w = ww[side, pl.ds(m, 1), :]
            return total + w * wf[side, pl.ds(base - lags[m], ERR), :]

        pred = lax.fori_loop(0, lags.shape[0], add, jnp.zeros((ERR, HALF), F32))
        eb[side] = jnp.where(inside, wf[side, pl.ds(pl.multiple_of(base, ROWS), ERR), :] - pred, 0.0)

    def ahead(side):
        def add(m, total):
            w = ww[side, pl.ds(m, 1), :]
            return total + w * eb[side, pl.ds(lags[m], ROWS), :]

        return lax.fori_loop(0, lags.shape[0], add, jnp.zeros((ROWS, HALF), F32))

    errors(0)

    for n, (i, j) in enumerate(NEAR):
        arrive(rx.at[n], t_x, n, at_near(i, j))
    total = pt[pl.ds(x * NH, NH), c].astype(F32)
    for n in range(len(NEAR)):
        total = total + rx[n].astype(F32)
    qx[...] = total
    send(qx.at[1 - h], rh, t_h, 0, (tm, s_far))

    for d in range(1, NY):
        arrive(yb.at[d - 1], sb_y, d - 1, at_y((y + d) % NY))
    total = pb[:, y].astype(F32)
    for d in range(1, NY):
        total = total + yb[d - 1].astype(F32)
    qb[...] = total
    qb16[...] = total.astype(BF16)
    for d in range(1, NZ):
        there = (z + d) % NZ
        send(qb16.at[there], zb.at[d - 1], sb_z, d - 1, at_z(there))
    for n, shift in enumerate(SHIFTS):
        for e in range(per_z if shift else 1):
            source = (own_block + SB - shift) % SB * per_z + e if shift else own_block * per_z + (z + 1) % per_z
            arrive(za.at[source], sa_z, (0, source), at_z(source))
    total = pa[z].astype(F32)
    for d in range(1, NZ):
        total = total + za[(z + d) % NZ].astype(F32)
    qa[...] = total
    for d in range(1, NY):
        there = (y + d) % NY
        send(qa.at[there], ya.at[d - 1], sa_y, d - 1, at_y(there))

    errors(1)
    grads = [2.0 * (eb[side, pl.ds(0, ROWS), :] - ahead(side)) for side in range(2)]
    arrive(rh, t_h, 0, (tm, s_far))
    own = qx[h] + rh[...]
    out[1] = own + jnp.concatenate(grads, axis=1)

    for d in range(1, NZ):
        arrive(zb.at[d - 1], sb_z, d - 1, at_z((z + d) % NZ))
    right = qb[z]
    for d in range(1, NZ):
        right = right + zb[d - 1].astype(F32)
    for d in range(1, NY):
        arrive(ya.at[d - 1], sa_y, d - 1, at_y((y + d) % NY))
    left = qa[y]
    for d in range(1, NY):
        left = left + ya[d - 1]
    out[0] = jnp.concatenate([left, right], axis=1)

    for one in sent:
        one.wait_send()

    @pl.when(gives_past)
    def _():
        give_past.wait_send()

    @pl.when(gives_next)
    def _():
        give_next.wait_send()


def shards(series_factors, time_factors, tile_values, tile_blocks, tile_counts, lags, lag_weights):
    vmem = pl.BlockSpec(memory_space=pltpu.VMEM)
    anywhere = pl.BlockSpec(memory_space=pl.ANY)
    slots = tile_values.shape[0]
    own = jax.ShapeDtypeStruct((2, ROWS, TILE), F32)

    def pair(n):
        return pltpu.SemaphoreType.DMA((2, n))

    both = pl.pallas_call(
            kernel,
            out_shape=own,
            in_specs=[anywhere] * 7,
            out_specs=vmem,
            scratch_shapes=[
                pltpu.VMEM((ROWS, TILE), BF16),
                pltpu.VMEM((ROWS, TILE), BF16),
                pltpu.SMEM((2, slots), jnp.int32),
                pltpu.SMEM((1,), jnp.int32),
                pltpu.SMEM(lags.shape, jnp.int32),
                pltpu.VMEM(lag_weights.shape, F32),
                pltpu.VMEM((slots, TILE, TILE), BF16),
                pltpu.VMEM((slots, TILE, TILE), BF16),
                pltpu.VMEM((NZ, NY, ROWS, HALF), BF16),
                pltpu.VMEM((NZ, NY, ROWS, HALF), BF16),
                pltpu.VMEM((SLAB // NC, NC, ROWS, TILE), BF16),
                pltpu.VMEM((HALO // NC, NC, ROWS, TILE), BF16),
                pltpu.VMEM((HALO // NC, NC, ROWS, TILE), BF16),
                pltpu.VMEM((slots, TILE, TILE), F32),
                pltpu.VMEM((slots, TILE, TILE), F32),
                pltpu.VMEM((NZ, NY, ROWS, HALF), BF16),
                pltpu.VMEM((NZ, NY, ROWS, HALF), BF16),
                pltpu.VMEM((SLAB // NC, NC, ROWS, TILE), BF16),
                pltpu.VMEM((NZ, NY, ROWS, HALF), BF16),
                pltpu.VMEM((NY - 1, NZ, ROWS, HALF), BF16),
                pltpu.VMEM((NY, ROWS, HALF), F32),
                pltpu.VMEM((NZ, ROWS, HALF), F32),
                pltpu.VMEM((NY - 1, ROWS, HALF), F32),
                pltpu.VMEM((NZ - 1, ROWS, HALF), BF16),
                pltpu.VMEM((NZ, ROWS, HALF), BF16),
                pltpu.VMEM((len(NEAR), NH, ROWS, TILE), BF16),
                pltpu.VMEM((NH, ROWS, TILE), F32),
                pltpu.VMEM((ROWS, TILE), F32),
                pltpu.VMEM((2, (SLAB + 2 * HALO) * ROWS, HALF), F32),
                pltpu.VMEM((2, ERR, HALF), F32),
                pltpu.VMEM((2, *lags.shape, HALF), F32),
                pltpu.SemaphoreType.DMA((7,)),
                pair(NY - 1), pair(NZ - 1), pair(NZ - 1), pair(NY - 1),
                pair(1), pair(len(NEAR)), pair(2),
                pair(NZ), pair(NY - 1), pair((NY - 1) * SB), pair(NZ - 1),
                pair(len(NEAR)), pair(1),
            ],
            compiler_params=pltpu.CompilerParams(
                collective_id=0, has_side_effects=True, vmem_limit_bytes=60 * 2**20
            ),
            cost_estimate=pl.CostEstimate(
                flops=slots * 6 * TILE**3, bytes_accessed=slots * 2 * TILE**2, transcendentals=0
            ),
        )(series_factors, time_factors, tile_values, tile_blocks.T, tile_counts, lags, lag_weights)
    return both[0] + 0.5 * series_factors.astype(F32), both[1] + 0.5 * time_factors.astype(F32)


def solution(mesh):
    placed = (
        P(("series", "tm"), None),
        P(("tm", "series"), None),
        P(("tm", "series"), None, None),
        P(("tm", "series"), None),
        P(("tm", "series")),
        P(),
        P(),
    )
    return jax.shard_map(
        shards,
        mesh=mesh,
        in_specs=placed,
        out_specs=(P(("series", "tm"), None), P(("tm", "series"), None)),
        check_vma=False,
    )
```
